32 devices in a mesh: gx: 4 (over z), gy: 8 (over y, x, core).
Axes of the slice: x: 2, y: 2, z: 4, core: 2. Of those that a mesh axis runs over, the one named last changes fastest.
Arguments:
- orbitals: float32 [2, 128, 128, 256], P(None, 'gx', 'gy'), may hold values from -6 to 6
- potential: float32 [128, 128, 256], P('gx', 'gy'), may hold values from -4 to 4
- projectors: float32 [1024, 9, 1024], P(('gx', 'gy')), may hold values from -3 to 3
- strengths: float32 [9], replicated, may hold values from 0.5 to 2
- atom_owner: int32 [640], replicated, may hold values from 0 to 31, as said below
- slot_atom: int32 [1024], P(('gx', 'gy')), may hold values from 0 to 640, as said below
- slot_offset: int32 [3, 1024], P(None, ('gx', 'gy')), may hold values from 0 to 240, as said below
Outputs:
- first_filter: float32 [2, 128, 128, 256], P(None, 'gx', 'gy')
- second_filter: float32 [2, 128, 128, 256], P(None, 'gx', 'gy')
The draws below stay inside these ranges and needn't reach their ends.
Inputs may be any that keep to these rules, and one draw needn't show every extreme that they name: `atom_owner`: every tile owns 1 to 39 atoms, and some tile owns exactly 39. `slot_atom`: every live slot is linked; the first slots of a tile are live and the rest empty; at most 32 live slots a tile, and some tile has empty slots. `slot_offset`: A patch lies within its tile: the first entry is at most 24, the second at most 8, the third at most 240, which some slot reaches.
All inputs are finite; a program needn't handle non-finite values.
Results may differ from the reference program's by a relative error of at most 0.00012.
Values sent between devices are 32-bit elements; how exact they have to be, the bound alone decides.
A program may use at most 64 MiB of HBM per device.

```python
import math
import jax
import jax.numpy as jnp
from jax import lax

CX = 32
CY = 16
NZ = 256
ATOM_DEV = 20
KSLOT = 32
ORB = 2
NPROJ = 9
BXY = 8
BZ = 16
BOX = 1024
ATOMS = 640
SLOTS = 1024
NX = 128
NY = 128
N_GX = 4
N_GY = 8


def owner_table(key):
    base_key = jax.random.fold_in(key, 101)
    device_count = N_GX * N_GY
    pair_count = device_count // 2
    key_moved, key_fullest, key_shuffle = jax.random.split(base_key, 3)
    moved = jax.random.randint(key_moved, (pair_count,), 0, ATOM_DEV)
    fullest = jax.random.randint(key_fullest, (), 0, pair_count)
    moved = jnp.where(jnp.arange(pair_count) == fullest, ATOM_DEV - 1, moved)
    places = jnp.arange(ATOMS, dtype=jnp.int32)
    tile_of = places // ATOM_DEV
    position = places % ATOM_DEV
    moved_back = (tile_of % 2 == 1) & (position < moved[tile_of // 2])
    tile_of = jnp.where(moved_back, tile_of - 1, tile_of)
    shuffle = jax.random.permutation(key_shuffle, ATOMS)
    return tile_of[shuffle].astype(jnp.int32)


def draw_atom_owner(key, part):
    return owner_table(key)


def draw_slot_atom(key, part):
    owner_tile = owner_table(key)
    device_count = N_GX * N_GY
    counts = jnp.sum((owner_tile[None, :] == jnp.arange(device_count)[:, None]).astype(jnp.int32), axis=1)
    starts = jnp.cumsum(counts) - counts
    sorted_atoms = jnp.argsort(owner_tile, stable=True).astype(jnp.int32)
    slot_key = jax.random.fold_in(key, 202)
    key_live, key_dir, key_rank, key_low = jax.random.split(slot_key, 4)
    live_count = jax.random.randint(key_live, (device_count,), KSLOT // 2, KSLOT + 1)
    lowest = jax.random.randint(key_low, (), 0, device_count)
    live_count = jnp.where(jnp.arange(device_count) == lowest, KSLOT // 2, live_count)
    device = jnp.arange(device_count)[:, None]
    slot_pos = jnp.arange(KSLOT)[None, :]
    direction = jax.random.randint(key_dir, (device_count, KSLOT), 0, 9)
    step_x = direction // 3 - 1
    step_y = direction % 3 - 1
    nearby = (device // N_GY + step_x) % N_GX * N_GY + (device % N_GY + step_y) % N_GY
    owner_rank = jax.random.randint(key_rank, (device_count, KSLOT), 0, counts[nearby])
    atoms_hit = sorted_atoms[starts[nearby] + owner_rank]
    atoms_hit = jnp.where(slot_pos < live_count[:, None], atoms_hit, ATOMS)
    return atoms_hit.reshape(-1).astype(jnp.int32)


def draw_slot_offset(key, part):
    total_slots = N_GX * N_GY * KSLOT
    offset_key = jax.random.fold_in(key, 303)
    key_x, key_y, key_z, key_pick = jax.random.split(offset_key, 4)
    corner_x = jax.random.randint(key_x, (total_slots,), 0, CX - BXY + 1)
    corner_y = jax.random.randint(key_y, (total_slots,), 0, CY - BXY + 1)
    corner_z = jax.random.randint(key_z, (total_slots,), 0, NZ - BZ + 1)
    picked = jax.random.randint(key_pick, (), 0, total_slots)
    corner_z = jnp.where(jnp.arange(total_slots) == picked, NZ - BZ, corner_z)
    corner_x = jnp.where(jnp.arange(total_slots) == picked, CX - BXY, corner_x)
    corner_y = jnp.where(jnp.arange(total_slots) == picked, CY - BXY, corner_y)
    return jnp.stack([corner_x, corner_y, corner_z]).astype(jnp.int32)


def block_levels(own_key, shape, cuts, smallest, largest):
    loudness, own = 1.0, jax.random.fold_in(own_key, 6)
    for dim, parts in cuts:
        steps = jnp.exp(jax.random.uniform(jax.random.fold_in(own, dim), (parts,), jnp.float32, smallest / len(cuts), largest / len(cuts)))
        loudness = loudness * jnp.repeat(steps, shape[dim] // parts).reshape([-1 if axis == dim else 1 for axis in range(len(shape))])
    return loudness


def gaussian(own_key, extent, scale, most, pieces=(), held_as=jnp.bfloat16):
    gain = block_levels(own_key, extent, pieces, -0.22, 0.18) if pieces else 1.0
    values = jax.random.normal(own_key, extent, jnp.float32) * scale * gain
    return jnp.minimum(jnp.maximum(values, -most), most).astype(held_as)


def setup_inputs(seed: int = 0) -> dict:
    splits = jax.random.split(jax.random.key(seed), 8)
    orbitals = gaussian(splits[0], (ORB, NX, NY, NZ), 1.0, 6.0, ((1, 4), (2, 8)), jnp.float32)
    potential = jnp.clip(jax.random.uniform(splits[1], (NX, NY, NZ), jnp.float32, -4.0, 4.0) * block_levels(splits[1], (NX, NY, NZ), ((0, 4), (1, 8)), -0.4, 0.0), -4.0, 4.0)
    projectors = gaussian(splits[2], (SLOTS, NPROJ, BOX), 0.5, 3.0, ((0, 32),), jnp.float32)
    strengths = jnp.clip(jnp.exp(jax.random.uniform(splits[3], (NPROJ,), jnp.float32, math.log(0.5), math.log(2.0))), 0.5, 2.0)
    atom_owner = draw_atom_owner(jax.random.fold_in(splits[7], 71), 0)
    slot_atom = draw_slot_atom(jax.random.fold_in(splits[7], 71), 0)
    slot_offset = draw_slot_offset(jax.random.fold_in(splits[7], 71), 0)
    return dict(orbitals=orbitals, potential=potential, projectors=projectors, strengths=strengths, atom_owner=atom_owner, slot_atom=slot_atom, slot_offset=slot_offset)


LAPLACE_COEFFS = (-5369.0 / 1800.0, 12.0 / 7.0, -15.0 / 56.0, 10.0 / 189.0, -1.0 / 112.0, 2.0 / 1925.0, -1.0 / 16632.0)
SPACING = 0.4
CENTER = 45.0
HALF_WIDTH = 48.0


def kinetic(orbital):
    depth = orbital.shape[3]
    padded_z = jnp.pad(orbital, ((0, 0), (0, 0), (0, 0), (6, 6)))
    summed = (3.0 * LAPLACE_COEFFS[0]) * orbital
    for reach in range(1, 7):
        paired = jnp.roll(orbital, reach, 1) + jnp.roll(orbital, -reach, 1)
        paired = paired + jnp.roll(orbital, reach, 2) + jnp.roll(orbital, -reach, 2)
        paired = paired + padded_z[:, :, :, 6 + reach:6 + reach + depth] + padded_z[:, :, :, 6 - reach:6 - reach + depth]
        summed = summed + LAPLACE_COEFFS[reach] * paired
    return (-0.5 / (SPACING * SPACING)) * summed


def patch_index(slot_offset, size_y, size_z):
    slot_count = slot_offset.shape[1]
    device = jnp.arange(slot_count, dtype=jnp.int32) // KSLOT
    corner_x = (device // N_GY) * CX + slot_offset[0]
    corner_y = (device % N_GY) * CY + slot_offset[1]
    cell_ids = jnp.arange(BOX, dtype=jnp.int32)
    step_x = cell_ids // (BXY * BZ)
    step_y = (cell_ids // BZ) % BXY
    step_z = cell_ids % BZ
    pos_x = corner_x[:, None] + step_x[None, :]
    pos_y = corner_y[:, None] + step_y[None, :]
    pos_z = slot_offset[2][:, None] + step_z[None, :]
    return ((pos_x * size_y + pos_y) * size_z + pos_z).astype(jnp.int32)


def linked_slots(atom_owner, slot_atom):
    slot_count = slot_atom.shape[0]
    device = jnp.arange(slot_count, dtype=jnp.int32) // KSLOT
    safe_atom = jnp.minimum(slot_atom, ATOMS - 1)
    owner_tile = atom_owner[safe_atom]
    step_x = (owner_tile // N_GY - device // N_GY + 1) % N_GX - 1
    step_y = (owner_tile % N_GY - device % N_GY + 1) % N_GY - 1
    return (slot_atom < ATOMS) & (step_x <= 1) & (step_y <= 1)


def nonlocal_term(orbital, projectors, strengths, slot_atom, linked, flat_index):
    flat_field = orbital.reshape(orbital.shape[0], -1)
    patches = flat_field[:, flat_index]
    partial_value = jnp.einsum("spc,osc->spo", projectors, patches, precision=lax.Precision.HIGHEST)
    target = jnp.where(linked, slot_atom, ATOMS).astype(jnp.int32)
    atom_table = jax.ops.segment_sum(partial_value * linked.astype(jnp.float32)[:, None, None], target, num_segments=ATOMS + 1)
    coefficient = atom_table[target] * linked.astype(jnp.float32)[:, None, None] * strengths[None, :, None]
    added = jnp.einsum("spc,spo->osc", projectors, coefficient, precision=lax.Precision.HIGHEST)
    result = jnp.zeros_like(flat_field).at[:, flat_index].add(added)
    return result.reshape(orbital.shape)


def reference(orbitals, potential, projectors, strengths, atom_owner, slot_atom, slot_offset):
    flat_index = patch_index(slot_offset, orbitals.shape[2], orbitals.shape[3])
    linked = linked_slots(atom_owner, slot_atom)

    def hamiltonian(orbital):
        return kinetic(orbital) + potential[None] * orbital + nonlocal_term(orbital, projectors, strengths, slot_atom, linked, flat_index)

    first_filter = (hamiltonian(orbitals) - CENTER * orbitals) / HALF_WIDTH
    second_filter = 2.0 * (hamiltonian(first_filter) - CENTER * first_filter) / HALF_WIDTH - orbitals
    return (first_filter, second_filter)
```

```python
import functools

import jax
import jax.numpy as jnp
from jax import lax
from jax.experimental import pallas as pl
from jax.experimental.pallas import tpu as pltpu
from jax.sharding import PartitionSpec as P

BXY = 8
BZ = 16
HALO = 6
GROUP = 4
MESH = pl.DeviceIdType.MESH
HIGHEST = lax.Precision.HIGHEST

LAPLACE_COEFFS = (
    -5369.0 / 1800.0,
    12.0 / 7.0,
    -15.0 / 56.0,
    10.0 / 189.0,
    -1.0 / 112.0,
    2.0 / 1925.0,
    -1.0 / 16632.0,
)
SPACING = 0.4
CENTER = 45.0
HALF_WIDTH = 48.0
KINETIC = -0.5 / (SPACING * SPACING)
VMEM_LIMIT = 40 * 1024 * 1024


def lane_windows(start):
    lanes = lax.broadcasted_iota(jnp.int32, (BXY, 128), 1)
    return [(lanes + h * 128 >= start) & (lanes + h * 128 < start + BZ) for h in range(2)]


def gather_partials(field_b, packed, offset, atom_row, sums, msg):
    slots, nproj = packed.shape[0], packed.shape[1]
    size_x = field_b.shape[2] // 2
    quantities = 2 * nproj
    rows = sums.shape[0]
    sums[quantities * slots :, :] = jnp.zeros((rows - quantities * slots, 128), jnp.float32)

    def body(s, _):
        x0, y0, z0 = offset[0, s], offset[1, s], offset[2, s]
        windows = lane_windows(z0)
        patches = []
        for o in range(2):
            total = None
            for b in range(BXY):
                rows = pl.ds(o * size_x + x0, BXY)
                plane = jnp.where(windows[0], field_b[y0 + b, 0, rows, :], 0.0)
                plane = jnp.where(windows[1], field_b[y0 + b, 1, rows, :], plane)
                plane = pltpu.roll(plane, (b * BZ + 256 - z0) & 127, 1)
                total = plane if total is None else total + plane
            patches.append(total)
        for p in range(nproj):
            values = packed[s, p]
            for o in range(2):
                row = jnp.sum(values * patches[o], axis=0, keepdims=True)
                sums[pl.ds((2 * p + o) * slots + s, 1), :] = row
        return 0

    lax.fori_loop(0, slots, body, 0, unroll=2)
    summed = lax.dot_general(
        jnp.ones((8, 128), jnp.float32),
        sums[...],
        (((1,), (1,)), ((), ())),
        precision=HIGHEST,
        preferred_element_type=jnp.float32,
    )
    row_ids = lax.broadcasted_iota(jnp.int32, (8, 128), 0)
    out = jnp.where(row_ids == 5, atom_row[...], 0.0)
    for r in range(5):
        out = jnp.where(row_ids == r, summed[:, r * 128 : (r + 1) * 128], out)
    msg[...] = out


def scatter_added(field_b, packed, offset, coef, strengths, scale):
    slots, nproj = packed.shape[0], packed.shape[1]
    size_x = field_b.shape[2] // 2

    def body(s, _):
        x0, y0, z0 = offset[0, s], offset[1, s], offset[2, s]
        windows = lane_windows(z0)
        added = [None, None]
        for p in range(nproj):
            values = packed[s, p]
            for o in range(2):
                q = 2 * p + o
                factor = coef[q // GROUP, (q % GROUP) * slots + s] * (strengths[0, p] * scale)
                term = values * factor
                added[o] = term if added[o] is None else added[o] + term
        for o in range(2):
            for b in range(BXY):
                moved = pltpu.roll(added[o], (z0 + 128 - b * BZ) & 127, 1)
                for h in range(2):
                    where = (y0 + b, h, pl.ds(o * size_x + x0, BXY), slice(None))
                    field_b[where] = field_b[where] + jnp.where(windows[h], moved, 0.0)
        return 0

    lax.fori_loop(0, slots, body, 0)


def first_kernel(orb, proj, atom_row, offset, field_b, packed, msg, sums):
    size_x, size_y = orb.shape[1], orb.shape[2]
    for o in range(2):
        for x in range(0, size_x, 8):
            turned = jnp.swapaxes(orb[o, x : x + 8], 0, 1)
            for h in range(2):
                rows = slice(o * size_x + x, o * size_x + x + 8)
                field_b[:, h, rows, :] = turned[:, :, h * 128 : (h + 1) * 128]
    slots = proj.shape[0]

    def pack(s, _):
        for a in range(BXY):
            packed[s, :, a, :] = proj[s, :, a * 128 : (a + 1) * 128]
        return 0

    lax.fori_loop(0, slots, pack, 0)
    gather_partials(field_b, packed, offset, atom_row, sums, msg)


def middle_kernel(
    base_a, base_b, packed, atom_row, offset, coef, strengths, out_a, out_b, msg, sums, *, scale
):
    size_x = base_a.shape[1]
    out_b[...] = base_b[...]
    scatter_added(out_b, packed, offset, coef, strengths, scale)
    for o in range(2):
        for x in range(0, size_x, 8):
            rows = slice(o * size_x + x, o * size_x + x + 8)
            for h in range(2):
                lanes = slice(h * 128, (h + 1) * 128)
                block = base_a[o, x : x + 8, :, lanes] + jnp.swapaxes(out_b[:, h, rows, :], 0, 1)
                out_a[o, x : x + 8, :, lanes] = block
                out_b[:, h, rows, :] = jnp.swapaxes(block, 0, 1)
    gather_partials(out_b, packed, offset, atom_row, sums, msg)


def last_kernel(base_a, base_b, packed, offset, coef, strengths, out_a, work, *, scale):
    size_x = base_a.shape[1]
    work[...] = base_b[...]
    scatter_added(work, packed, offset, coef, strengths, scale)
    for o in range(2):
        for x in range(0, size_x, 8):
            rows = slice(o * size_x + x, o * size_x + x + 8)
            for h in range(2):
                lanes = slice(h * 128, (h + 1) * 128)
                block = base_a[o, x : x + 8, :, lanes] + jnp.swapaxes(work[:, h, rows, :], 0, 1)
                out_a[o, x : x + 8, :, lanes] = block


def partner_offsets(devices):
    if devices >= 5:
        return (0, 1, 2, devices - 2, devices - 1)
    return tuple(range(devices))


def exchange_kernel(*refs, scale, subtract, grid_x, grid_y):
    if subtract:
        field, field_b, pot, msg, atom_col, previous = refs[:6]
        refs = refs[6:]
    else:
        field, field_b, pot, msg, atom_col = refs[:5]
        refs = refs[5:]
    base_a, base_b, coef, pad_a, pad_b, inbox, halo_send, halo_recv, msg_send, msg_recv = refs
    size_x, size_y, depth = field.shape[1], field.shape[2], field.shape[3]
    me_x, me_y = lax.axis_index("gx"), lax.axis_index("gy")
    steps = [
        (dx, dy)
        for dx in partner_offsets(grid_x)
        for dy in partner_offsets(grid_y)
        if (dx, dy) != (0, 0)
    ]

    def device(dx, dy):
        return (lax.rem(me_x + dx, grid_x), lax.rem(me_y + dy, grid_y))

    barrier = pltpu.get_barrier_semaphore()
    for dx, dy in steps:
        pl.semaphore_signal(barrier, inc=1, device_id=device(dx, dy), device_id_type=MESH)
    pl.semaphore_wait(barrier, len(steps))

    halos = []
    for i, (src, dst, target) in enumerate(
        (
            (
                field_b.at[pl.ds(size_y - HALO, HALO)],
                pad_b.at[pl.ds(0, HALO)],
                device(0, 1),
            ),
            (
                field_b.at[pl.ds(0, HALO)],
                pad_b.at[pl.ds(HALO + size_y, HALO)],
                device(0, grid_y - 1),
            ),
            (
                field.at[:, pl.ds(size_x - HALO, HALO)],
                pad_a.at[:, pl.ds(0, HALO)],
                device(1, 0),
            ),
            (
                field.at[:, pl.ds(0, HALO)],
                pad_a.at[:, pl.ds(HALO + size_x, HALO)],
                device(grid_x - 1, 0),
            ),
        )
    ):
        halos.append(
            pltpu.make_async_remote_copy(
                src_ref=src,
                dst_ref=dst,
                send_sem=halo_send.at[i],
                recv_sem=halo_recv.at[i],
                device_id=target,
                device_id_type=MESH,
            )
        )
    letters = []
    for i, (dx, dy) in enumerate(steps):
        letters.append(
            pltpu.make_async_remote_copy(
                src_ref=msg,
                dst_ref=inbox.at[i],
                send_sem=msg_send.at[i],
                recv_sem=msg_recv.at[i],
                device_id=device(dx, dy),
                device_id_type=MESH,
            )
        )
    for copy in halos:
        copy.start()
    for copy in letters:
        copy.start()

    factor = KINETIC * scale
    row = lax.broadcasted_iota(jnp.int32, (depth, depth), 0)
    column = lax.broadcasted_iota(jnp.int32, (depth, depth), 1)
    apart = jnp.abs(row - column)
    band = jnp.where(apart == 0, 3.0 * LAPLACE_COEFFS[0] * factor - CENTER * scale, 0.0)
    for reach in range(1, HALO + 1):
        band = jnp.where(apart == reach, LAPLACE_COEFFS[reach] * factor, band)
    width = 8

    def own(i, _):
        xs = pl.ds(i * width, width)
        local = pot[xs] * scale
        for o in range(2):
            block = field[o, xs]
            along_z = lax.dot_general(
                block.reshape(width * size_y, depth),
                band,
                (((1,), (0,)), ((), ())),
                precision=HIGHEST,
                preferred_element_type=jnp.float32,
            ).reshape(width, size_y, depth)
            total = along_z + local * block
            if subtract:
                total = total - previous[o, xs]
            base_a[o, xs] = total
            pad_a[o, pl.ds(HALO + i * width, width)] = block
        return 0

    lax.fori_loop(0, size_x // width, own, 0)
    pad_b[HALO : HALO + size_y] = field_b[...]

    group_r = lax.broadcasted_iota(jnp.int32, (128, 128), 0) // 32
    group_c = lax.broadcasted_iota(jnp.int32, (128, 128), 1) // 32
    same_group = group_r == group_c
    mine = atom_col[...]

    def matched(letter):
        same = same_group & (mine == letter[5:6, :])
        return lax.dot_general(
            letter,
            same.astype(jnp.float32),
            (((1,), (1,)), ((), ())),
            precision=HIGHEST,
            preferred_element_type=jnp.float32,
        )

    for copy in letters:
        copy.wait()
    coef[...] = matched(msg[...])

    def add_letter(i, _):
        coef[...] = coef[...] + matched(inbox[i])
        return 0

    lax.fori_loop(0, len(steps), add_letter, 0)

    for copy in halos[2:]:
        copy.wait()

    def along_x(x, _):
        for o in range(2):
            total = base_a[o, x]
            for reach in range(1, HALO + 1):
                pair = pad_a[o, x + HALO + reach] + pad_a[o, x + HALO - reach]
                total = total + (LAPLACE_COEFFS[reach] * factor) * pair
            base_a[o, x] = total
        return 0

    lax.fori_loop(0, size_x, along_x, 0)
    for copy in halos[:2]:
        copy.wait()

    def along_y(y, _):
        for h in range(2):
            total = None
            for reach in range(1, HALO + 1):
                pair = pad_b[y + HALO + reach, h] + pad_b[y + HALO - reach, h]
                term = (LAPLACE_COEFFS[reach] * factor) * pair
                total = term if total is None else total + term
            base_b[y, h] = total
        return 0

    lax.fori_loop(0, size_y, along_y, 0)


def shards(
    orbitals, potential, projectors, strengths, atom_owner, slot_atom, slot_offset, grid_x, grid_y
):
    orbit, size_x, size_y, depth = orbitals.shape
    slots, nproj, box = projectors.shape
    f32 = jnp.float32
    vmem = pl.BlockSpec(memory_space=pltpu.VMEM)
    smem = pl.BlockSpec(memory_space=pltpu.SMEM)
    shape_a = jax.ShapeDtypeStruct(orbitals.shape, f32)
    shape_b = jax.ShapeDtypeStruct((size_y, 2, orbit * size_x, depth // 2), f32)
    shape_p = jax.ShapeDtypeStruct((slots, nproj, BXY, 128), f32)
    shape_m = jax.ShapeDtypeStruct((8, 128), f32)
    sums = pltpu.VMEM((20 * slots, 128), f32)

    live = slot_atom < atom_owner.shape[0]
    numbers = slot_atom.astype(f32)
    atom_row = jnp.tile(jnp.where(live, numbers, -1.0), GROUP)
    atom_row = jnp.broadcast_to(atom_row[None, :], (8, 128))
    atom_col = jnp.tile(jnp.where(live, numbers, -2.0), GROUP)
    atom_col = jnp.broadcast_to(atom_col[:, None], (128, 128))
    strengths = strengths.reshape(1, nproj)
    plain = pltpu.CompilerParams(vmem_limit_bytes=VMEM_LIMIT)

    field_b, packed, msg = pl.pallas_call(
        first_kernel,
        out_shape=(shape_b, shape_p, shape_m),
        in_specs=[vmem, vmem, vmem, smem],
        out_specs=(vmem, vmem, vmem),
        scratch_shapes=[sums],
        compiler_params=plain,
        name="gather_partials",
    )(orbitals, projectors, atom_row, slot_offset)

    steps = len(partner_offsets(grid_x)) * len(partner_offsets(grid_y)) - 1

    def exchange(field, field_b, msg, previous, scale, number):
        args = [field, field_b, potential, msg, atom_col]
        if previous is not None:
            args.append(previous)
        return pl.pallas_call(
            functools.partial(
                exchange_kernel,
                scale=scale,
                subtract=previous is not None,
                grid_x=grid_x,
                grid_y=grid_y,
            ),
            out_shape=(shape_a, shape_b, shape_m),
            in_specs=[vmem] * len(args),
            out_specs=(vmem, vmem, vmem),
            scratch_shapes=[
                pltpu.VMEM((orbit, size_x + 2 * HALO, size_y, depth), f32),
                pltpu.VMEM((size_y + 2 * HALO, 2, orbit * size_x, depth // 2), f32),
                pltpu.VMEM((steps, 8, 128), f32),
                pltpu.SemaphoreType.DMA((4,)),
                pltpu.SemaphoreType.DMA((4,)),
                pltpu.SemaphoreType.DMA((steps,)),
                pltpu.SemaphoreType.DMA((steps,)),
            ],
            compiler_params=pltpu.CompilerParams(
                collective_id=number, has_side_effects=True, vmem_limit_bytes=VMEM_LIMIT
            ),
            name="exchange_%d" % number,
        )(*args)

    base_a, base_b, coef = exchange(orbitals, field_b, msg, None, 1.0 / HALF_WIDTH, 0)
    first, field_b, msg = pl.pallas_call(
        functools.partial(middle_kernel, scale=1.0 / HALF_WIDTH),
        out_shape=(shape_a, shape_b, shape_m),
        in_specs=[vmem, vmem, vmem, vmem, smem, smem, smem],
        out_specs=(vmem, vmem, vmem),
        scratch_shapes=[sums],
        compiler_params=plain,
        name="scatter_gather",
    )(base_a, base_b, packed, atom_row, slot_offset, coef, strengths)
    base_a, base_b, coef = exchange(first, field_b, msg, orbitals, 2.0 / HALF_WIDTH, 1)
    second = pl.pallas_call(
        functools.partial(last_kernel, scale=2.0 / HALF_WIDTH),
        out_shape=shape_a,
        in_specs=[vmem, vmem, vmem, smem, smem, smem],
        out_specs=vmem,
        scratch_shapes=[pltpu.VMEM((size_y, 2, orbit * size_x, depth // 2), f32)],
        compiler_params=plain,
        name="scatter_last",
    )(base_a, base_b, packed, slot_offset, coef, strengths)
    return (first, second)


def solution(mesh):
    return jax.shard_map(
        functools.partial(shards, grid_x=mesh.shape["gx"], grid_y=mesh.shape["gy"]),
        mesh=mesh,
        in_specs=(
            P(None, "gx", "gy", None),
            P("gx", "gy", None),
            P(("gx", "gy"), None, None),
            P(),
            P(),
            P(("gx", "gy")),
            P(None, ("gx", "gy")),
        ),
        out_specs=(P(None, "gx", "gy", None), P(None, "gx", "gy", None)),
        check_vma=False,
    )
```

```python
import functools

import jax
import jax.numpy as jnp
from jax import lax
from jax.experimental import pallas as pl
from jax.experimental.pallas import tpu as pltpu
from jax.sharding import PartitionSpec as P

BXY = 8
BZ = 16
HALO = 6
GROUP = 4
MESH = pl.DeviceIdType.MESH
HIGHEST = lax.Precision.HIGHEST

LAPLACE_COEFFS = (
    -5369.0 / 1800.0,
    12.0 / 7.0,
    -15.0 / 56.0,
    10.0 / 189.0,
    -1.0 / 112.0,
    2.0 / 1925.0,
    -1.0 / 16632.0,
)
SPACING = 0.4
CENTER = 45.0
HALF_WIDTH = 48.0
KINETIC = -0.5 / (SPACING * SPACING)
VMEM_LIMIT = 40 * 1024 * 1024


def lane_windows(start):
    lanes = lax.broadcasted_iota(jnp.int32, (BXY, 128), 1)
    return [(lanes + h * 128 >= start) & (lanes + h * 128 < start + BZ) for h in range(2)]


def gather_partials(field_b, packed, offset, atom_row, sums, msg):
    slots, nproj = packed.shape[0], packed.shape[1]
    size_x = field_b.shape[2] // 2
    quantities = 2 * nproj
    rows = sums.shape[0]
    sums[quantities * slots :, :] = jnp.zeros((rows - quantities * slots, 128), jnp.float32)

    def body(s, _):
        x0, y0, z0 = offset[0, s], offset[1, s], offset[2, s]
        windows = lane_windows(z0)
        patches = []
        for o in range(2):
            total = None
            for b in range(BXY):
                rows = pl.ds(o * size_x + x0, BXY)
                plane = jnp.where(windows[0], field_b[y0 + b, 0, rows, :], 0.0)
                plane = jnp.where(windows[1], field_b[y0 + b, 1, rows, :], plane)
                plane = pltpu.roll(plane, (b * BZ + 256 - z0) & 127, 1)
                total = plane if total is None else total + plane
            patches.append(total)
        found = []
        for p in range(nproj):
            values = packed[s, p]
            for o in range(2):
                found.append(jnp.sum(values * patches[o], axis=0, keepdims=True))
        for q, row in enumerate(found):
            sums[pl.ds(q * slots + s, 1), :] = row
        return 0

    lax.fori_loop(0, slots, body, 0, unroll=2)
    summed = lax.dot_general(
        jnp.ones((8, 128), jnp.float32),
        sums[...],
        (((1,), (1,)), ((), ())),
        precision=HIGHEST,
        preferred_element_type=jnp.float32,
    )
    row_ids = lax.broadcasted_iota(jnp.int32, (8, 128), 0)
    out = jnp.where(row_ids == 5, atom_row[...], 0.0)
    for r in range(5):
        out = jnp.where(row_ids == r, summed[:, r * 128 : (r + 1) * 128], out)
    msg[...] = out


def scatter_added(field_b, packed, offset, coef, strengths, scale):
    slots, nproj = packed.shape[0], packed.shape[1]
    size_x = field_b.shape[2] // 2

    def body(s, _):
        x0, y0, z0 = offset[0, s], offset[1, s], offset[2, s]
        windows = lane_windows(z0)
        added = [None, None]
        for p in range(nproj):
            values = packed[s, p]
            for o in range(2):
                q = 2 * p + o
                factor = coef[q // GROUP, (q % GROUP) * slots + s] * (strengths[0, p] * scale)
                term = values * factor
                added[o] = term if added[o] is None else added[o] + term
        places = [
            (o, b, h, (y0 + b, h, pl.ds(o * size_x + x0, BXY), slice(None)))
            for o in range(2)
            for b in range(BXY)
            for h in range(2)
        ]
        before = [field_b[where] for _, _, _, where in places]
        moved = [
            [pltpu.roll(added[o], (z0 + 128 - b * BZ) & 127, 1) for b in range(BXY)]
            for o in range(2)
        ]
        after = [
            old + jnp.where(windows[h], moved[o][b], 0.0)
            for old, (o, b, h, _) in zip(before, places)
        ]
        for value, (_, _, _, where) in zip(after, places):
            field_b[where] = value
        return 0

    lax.fori_loop(0, slots, body, 0, unroll=2)


def first_kernel(orb, proj, atom_row, offset, field_b, packed, msg, sums):
    size_x, size_y = orb.shape[1], orb.shape[2]
    for o in range(2):
        for x in range(0, size_x, 8):
            turned = jnp.swapaxes(orb[o, x : x + 8], 0, 1)
            for h in range(2):
                rows = slice(o * size_x + x, o * size_x + x + 8)
                field_b[:, h, rows, :] = turned[:, :, h * 128 : (h + 1) * 128]
    slots = proj.shape[0]

    def pack(s, _):
        for a in range(BXY):
            packed[s, :, a, :] = proj[s, :, a * 128 : (a + 1) * 128]
        return 0

    lax.fori_loop(0, slots, pack, 0)
    gather_partials(field_b, packed, offset, atom_row, sums, msg)


def middle_kernel(
    base_a, base_b, packed, atom_row, offset, coef, strengths, out_a, out_b, msg, sums, *, scale
):
    size_x = base_a.shape[1]
    out_b[...] = base_b[...]
    scatter_added(out_b, packed, offset, coef, strengths, scale)
    for o in range(2):
        for x in range(0, size_x, 8):
            rows = slice(o * size_x + x, o * size_x + x + 8)
            for h in range(2):
                lanes = slice(h * 128, (h + 1) * 128)
                block = base_a[o, x : x + 8, :, lanes] + jnp.swapaxes(out_b[:, h, rows, :], 0, 1)
                out_a[o, x : x + 8, :, lanes] = block
                out_b[:, h, rows, :] = jnp.swapaxes(block, 0, 1)
    gather_partials(out_b, packed, offset, atom_row, sums, msg)


def last_kernel(base_a, base_b, packed, offset, coef, strengths, out_a, work, *, scale):
    size_x = base_a.shape[1]
    work[...] = base_b[...]
    scatter_added(work, packed, offset, coef, strengths, scale)
    for o in range(2):
        for x in range(0, size_x, 8):
            rows = slice(o * size_x + x, o * size_x + x + 8)
            for h in range(2):
                lanes = slice(h * 128, (h + 1) * 128)
                block = base_a[o, x : x + 8, :, lanes] + jnp.swapaxes(work[:, h, rows, :], 0, 1)
                out_a[o, x : x + 8, :, lanes] = block


def partner_offsets(devices):
    if devices >= 5:
        return (0, 1, 2, devices - 2, devices - 1)
    return tuple(range(devices))


def exchange_kernel(*refs, scale, subtract, grid_x, grid_y):
    if subtract:
        field, field_b, pot, msg, atom_col, previous = refs[:6]
        refs = refs[6:]
    else:
        field, field_b, pot, msg, atom_col = refs[:5]
        refs = refs[5:]
    base_a, base_b, coef, pad_a, pad_b, inbox, halo_send, halo_recv, msg_send, msg_recv = refs
    size_x, size_y, depth = field.shape[1], field.shape[2], field.shape[3]
    me_x, me_y = lax.axis_index("gx"), lax.axis_index("gy")
    steps = [
        (dx, dy)
        for dx in partner_offsets(grid_x)
        for dy in partner_offsets(grid_y)
        if (dx, dy) != (0, 0)
    ]

    def device(dx, dy):
        return (lax.rem(me_x + dx, grid_x), lax.rem(me_y + dy, grid_y))

    barrier = pltpu.get_barrier_semaphore()
    for dx, dy in steps:
        pl.semaphore_signal(barrier, inc=1, device_id=device(dx, dy), device_id_type=MESH)
    pl.semaphore_wait(barrier, len(steps))

    halos = []
    for i, (src, dst, target) in enumerate(
        (
            (
                field_b.at[pl.ds(size_y - HALO, HALO)],
                pad_b.at[pl.ds(0, HALO)],
                device(0, 1),
            ),
            (
                field_b.at[pl.ds(0, HALO)],
                pad_b.at[pl.ds(HALO + size_y, HALO)],
                device(0, grid_y - 1),
            ),
            (
                field.at[:, pl.ds(size_x - HALO, HALO)],
                pad_a.at[:, pl.ds(0, HALO)],
                device(1, 0),
            ),
            (
                field.at[:, pl.ds(0, HALO)],
                pad_a.at[:, pl.ds(HALO + size_x, HALO)],
                device(grid_x - 1, 0),
            ),
        )
    ):
        halos.append(
            pltpu.make_async_remote_copy(
                src_ref=src,
                dst_ref=dst,
                send_sem=halo_send.at[i],
                recv_sem=halo_recv.at[i],
                device_id=target,
                device_id_type=MESH,
            )
        )
    letters = []
    for i, (dx, dy) in enumerate(steps):
        letters.append(
            pltpu.make_async_remote_copy(
                src_ref=msg,
                dst_ref=inbox.at[i],
                send_sem=msg_send.at[i],
                recv_sem=msg_recv.at[i],
                device_id=device(dx, dy),
                device_id_type=MESH,
            )
        )
    for copy in letters:
        copy.start()
    for copy in halos:
        copy.start()

    factor = KINETIC * scale
    row = lax.broadcasted_iota(jnp.int32, (depth, depth), 0)
    column = lax.broadcasted_iota(jnp.int32, (depth, depth), 1)
    apart = jnp.abs(row - column)
    band = jnp.where(apart == 0, 3.0 * LAPLACE_COEFFS[0] * factor - CENTER * scale, 0.0)
    for reach in range(1, HALO + 1):
        band = jnp.where(apart == reach, LAPLACE_COEFFS[reach] * factor, band)
    width = 8

    def own(i, _):
        xs = pl.ds(i * width, width)
        local = pot[xs] * scale
        for o in range(2):
            block = field[o, xs]
            along_z = lax.dot_general(
                block.reshape(width * size_y, depth),
                band,
                (((1,), (0,)), ((), ())),
                precision=HIGHEST,
                preferred_element_type=jnp.float32,
            ).reshape(width, size_y, depth)
            total = along_z + local * block
            if subtract:
                total = total - previous[o, xs]
            base_a[o, xs] = total
            pad_a[o, pl.ds(HALO + i * width, width)] = block
        return 0

    lax.fori_loop(0, size_x // width, own, 0)
    pad_b[HALO : HALO + size_y] = field_b[...]

    group_r = lax.broadcasted_iota(jnp.int32, (128, 128), 0) // 32
    group_c = lax.broadcasted_iota(jnp.int32, (128, 128), 1) // 32
    same_group = group_r == group_c
    mine = atom_col[...]

    def matched(letter):
        same = same_group & (mine == letter[5:6, :])
        high = letter.astype(jnp.bfloat16).astype(jnp.float32)
        rest = letter - high
        middle = rest.astype(jnp.bfloat16).astype(jnp.float32)
        terms = jnp.concatenate([high, middle, rest - middle, jnp.zeros_like(letter)], axis=0)
        return lax.dot_general(
            terms.astype(jnp.bfloat16),
            jnp.where(same, 1.0, 0.0).astype(jnp.bfloat16),
            (((1,), (1,)), ((), ())),
            preferred_element_type=jnp.float32,
        )

    def along_x(x, _):
        for o in range(2):
            total = base_a[o, x]
            for reach in range(1, HALO + 1):
                pair = pad_a[o, x + HALO + reach] + pad_a[o, x + HALO - reach]
                total = total + (LAPLACE_COEFFS[reach] * factor) * pair
            base_a[o, x] = total
        return 0

    def along_y(y, _):
        for h in range(2):
            total = None
            for reach in range(1, HALO + 1):
                pair = pad_b[y + HALO + reach, h] + pad_b[y + HALO - reach, h]
                term = (LAPLACE_COEFFS[reach] * factor) * pair
                total = term if total is None else total + term
            base_b[y, h] = total
        return 0

    lax.fori_loop(HALO, size_x - HALO, along_x, 0)
    lax.fori_loop(HALO, size_y - HALO, along_y, 0)

    for copy in letters:
        copy.wait()
    total = matched(msg[...])
    for i in range(len(steps)):
        total = total + matched(inbox[i])
    coef[...] = total[0:8] + total[8:16] + total[16:24]

    halos[2].wait()
    lax.fori_loop(0, HALO, along_x, 0)
    halos[3].wait()
    lax.fori_loop(size_x - HALO, size_x, along_x, 0)
    halos[0].wait()
    lax.fori_loop(0, HALO, along_y, 0)
    halos[1].wait()
    lax.fori_loop(size_y - HALO, size_y, along_y, 0)


def shards(
    orbitals, potential, projectors, strengths, atom_owner, slot_atom, slot_offset, grid_x, grid_y
):
    orbit, size_x, size_y, depth = orbitals.shape
    slots, nproj, box = projectors.shape
    f32 = jnp.float32
    vmem = pl.BlockSpec(memory_space=pltpu.VMEM)
    smem = pl.BlockSpec(memory_space=pltpu.SMEM)
    shape_a = jax.ShapeDtypeStruct(orbitals.shape, f32)
    shape_b = jax.ShapeDtypeStruct((size_y, 2, orbit * size_x, depth // 2), f32)
    shape_p = jax.ShapeDtypeStruct((slots, nproj, BXY, 128), f32)
    shape_m = jax.ShapeDtypeStruct((8, 128), f32)
    sums = pltpu.VMEM((20 * slots, 128), f32)

    live = slot_atom < atom_owner.shape[0]
    numbers = slot_atom.astype(f32)
    atom_row = jnp.tile(jnp.where(live, numbers, -1.0), GROUP)
    atom_row = jnp.broadcast_to(atom_row[None, :], (8, 128))
    atom_col = jnp.tile(jnp.where(live, numbers, -2.0), GROUP)
    atom_col = jnp.broadcast_to(atom_col[:, None], (128, 128))
    strengths = strengths.reshape(1, nproj)
    plain = pltpu.CompilerParams(vmem_limit_bytes=VMEM_LIMIT)

    field_b, packed, msg = pl.pallas_call(
        first_kernel,
        out_shape=(shape_b, shape_p, shape_m),
        in_specs=[vmem, vmem, vmem, smem],
        out_specs=(vmem, vmem, vmem),
        scratch_shapes=[sums],
        compiler_params=plain,
        name="gather_partials",
    )(orbitals, projectors, atom_row, slot_offset)

    steps = len(partner_offsets(grid_x)) * len(partner_offsets(grid_y)) - 1

    def exchange(field, field_b, msg, previous, scale, number):
        args = [field, field_b, potential, msg, atom_col]
        if previous is not None:
            args.append(previous)
        return pl.pallas_call(
            functools.partial(
                exchange_kernel,
                scale=scale,
                subtract=previous is not None,
                grid_x=grid_x,
                grid_y=grid_y,
            ),
            out_shape=(shape_a, shape_b, shape_m),
            in_specs=[vmem] * len(args),
            out_specs=(vmem, vmem, vmem),
            scratch_shapes=[
                pltpu.VMEM((orbit, size_x + 2 * HALO, size_y, depth), f32),
                pltpu.VMEM((size_y + 2 * HALO, 2, orbit * size_x, depth // 2), f32),
                pltpu.VMEM((steps, 8, 128), f32),
                pltpu.SemaphoreType.DMA((4,)),
                pltpu.SemaphoreType.DMA((4,)),
                pltpu.SemaphoreType.DMA((steps,)),
                pltpu.SemaphoreType.DMA((steps,)),
            ],
            compiler_params=pltpu.CompilerParams(
                collective_id=number, has_side_effects=True, vmem_limit_bytes=VMEM_LIMIT
            ),
            name="exchange_%d" % number,
        )(*args)

    base_a, base_b, coef = exchange(orbitals, field_b, msg, None, 1.0 / HALF_WIDTH, 0)
    first, field_b, msg = pl.pallas_call(
        functools.partial(middle_kernel, scale=1.0 / HALF_WIDTH),
        out_shape=(shape_a, shape_b, shape_m),
        in_specs=[vmem, vmem, vmem, vmem, smem, smem, smem],
        out_specs=(vmem, vmem, vmem),
        scratch_shapes=[sums],
        compiler_params=plain,
        name="scatter_gather",
    )(base_a, base_b, packed, atom_row, slot_offset, coef, strengths)
    base_a, base_b, coef = exchange(first, field_b, msg, orbitals, 2.0 / HALF_WIDTH, 1)
    second = pl.pallas_call(
        functools.partial(last_kernel, scale=2.0 / HALF_WIDTH),
        out_shape=shape_a,
        in_specs=[vmem, vmem, vmem, smem, smem, smem],
        out_specs=vmem,
        scratch_shapes=[pltpu.VMEM((size_y, 2, orbit * size_x, depth // 2), f32)],
        compiler_params=plain,
        name="scatter_last",
    )(base_a, base_b, packed, slot_offset, coef, strengths)
    return (first, second)


def solution(mesh):
    return jax.shard_map(
        functools.partial(shards, grid_x=mesh.shape["gx"], grid_y=mesh.shape["gy"]),
        mesh=mesh,
        in_specs=(
            P(None, "gx", "gy", None),
            P("gx", "gy", None),
            P(("gx", "gy"), None, None),
            P(),
            P(),
            P(("gx", "gy")),
            P(None, ("gx", "gy")),
        ),
        out_specs=(P(None, "gx", "gy", None), P(None, "gx", "gy", None)),
        check_vma=False,
    )
```
